256 devices in a mesh: blk: 64 (over x, y, z_lo, core), head: 4 (over z_hi).
Axes of the slice: x: 4, y: 4, z: 8 (z_hi: 4, z_lo: 2; z = z_hi * 2 + z_lo), core: 2. Of those that a mesh axis runs over, the one named last changes fastest.
Arguments:
- queries: bfloat16 [16384, 4096], P(('blk', 'head')), may hold values from -6 to 6
- keys: bfloat16 [16384, 512], P(('blk', 'head')), may hold values from -6 to 6
- values: bfloat16 [16384, 512], P(('blk', 'head')), may hold values from -6 to 6
- positions: int32 [16384], P(('blk', 'head')), may hold values from 0 to 16383, as said below
Outputs:
- attended: bfloat16 [16384, 4096], P(('blk', 'head'))
The draws below stay inside these ranges and needn't reach their ends.
Inputs may be any that keep to these rules, and one draw needn't show every extreme that they name: Positions are distinct. The rows fall into spans of 128 rows holding consecutive rising positions that start at a multiple of 128; the two spans of one index of blk are span j and span 2 * 64 - 1 - j of the document, each j at exactly one index. Positions are integer bookkeeping: any lossless encoding of them between devices is allowed.
All inputs are finite; a program needn't handle non-finite values.
Results may differ from the reference program's by a relative error of at most 0.0083.
Values may be sent and summed in bfloat16 or wider, within the bound.
A program may use at most 128 MiB of HBM per device.

```python
import math
import jax
import jax.numpy as jnp
import numpy as np
from jax import lax

QHEADS = 32
KVHEADS = 4
HEAD_DIM = 128
TOKENS = 16384
SPAN = 128
PAIRS = 64


def paired_draw(key):
    query_key = jax.random.fold_in(key, 101)
    other_key = jax.random.fold_in(key, 102)
    query_shape = (TOKENS, QHEADS * HEAD_DIM)
    key_shape = (TOKENS, KVHEADS * HEAD_DIM)
    query_base = jax.random.truncated_normal(query_key, -6.0, 6.0, query_shape, jnp.float32)
    key_base = jax.random.truncated_normal(other_key, -6.0, 6.0, key_shape, jnp.float32)
    return (query_base, key_base)


def draw_queries(key, part):
    return paired_draw(key)[0].astype(jnp.bfloat16)


def draw_keys(key, part):
    return paired_draw(key)[1].astype(jnp.bfloat16)


def draw_positions(key, part):
    order = jax.random.permutation(jax.random.fold_in(key, 201), PAIRS).astype(jnp.int32)
    rows = jnp.arange(TOKENS, dtype=jnp.int32)
    owner = rows // (2 * SPAN)
    within = rows % (2 * SPAN)
    picked = order[owner]
    span_index = jnp.where(within < SPAN, picked, 2 * PAIRS - 1 - picked)
    return (span_index * SPAN + within % SPAN).astype(jnp.int32)


def level_of(stream_key, extent, cuts, least, top_value):
    loudness = 1.0
    for dim, parts in cuts:
        steps = jax.random.uniform(jax.random.fold_in(jax.random.fold_in(stream_key, 6), dim), (parts,), jnp.float32, least / len(cuts), top_value / len(cuts))
        loudness = loudness * jnp.repeat(jnp.exp(steps), extent[dim] // parts).reshape((-1,) + (1,) * (len(extent) - 1 - dim))
    return loudness


def scatter_about(stream_key, dims, deviation, most, shards=(), kind=jnp.bfloat16):
    factor_of = level_of(stream_key, dims, shards, -0.22, 0.18) if shards else 1.0
    values = jax.random.normal(stream_key, dims, jnp.float32) * deviation * factor_of
    return jnp.minimum(jnp.maximum(values, -most), most).astype(kind)


def setup_inputs(seed: int = 0) -> dict:
    arg_keys = jax.random.split(jax.random.key(seed), 5)
    return {
        "queries": draw_queries(jax.random.fold_in(arg_keys[4], 71), 0),
        "keys": draw_keys(jax.random.fold_in(arg_keys[4], 71), 0),
        "values": scatter_about(arg_keys[2], (TOKENS, KVHEADS * HEAD_DIM), 1.0, 6.0, ((0, 256),)),
        "positions": draw_positions(jax.random.fold_in(arg_keys[4], 71), 0),
    }


def rope_table(size):
    entries = []
    for number in range(size // 2):
        inverse = 1.0 / (500000.0 ** (2.0 * number / size))
        wavelength = 2.0 * math.pi / inverse
        if wavelength < 2048.0:
            entries.append(inverse)
        elif wavelength > 8192.0:
            entries.append(inverse / 8.0)
        else:
            smooth = (8192.0 / wavelength - 1.0) / 3.0
            entries.append((1.0 - smooth) * inverse / 8.0 + smooth * inverse)
    return np.array(entries, dtype=np.float32)


def rotate(inputs, places, head_count):
    size = inputs.shape[1] // head_count
    table = jnp.asarray(rope_table(size))
    angles = places.astype(jnp.float32)[:, None] * table[None, :]
    cosine = jnp.cos(angles)[:, None, :]
    sine = jnp.sin(angles)[:, None, :]
    shaped = inputs.astype(jnp.float32).reshape(inputs.shape[0], head_count, size)
    half_size = size // 2
    first = shaped[:, :, :half_size]
    second = shaped[:, :, half_size:]
    turned = jnp.concatenate([first * cosine - second * sine, second * cosine + first * sine], axis=2)
    return turned.reshape(inputs.shape).astype(jnp.bfloat16)


def reference(queries, keys, values, positions):
    q_rot = rotate(queries, positions, QHEADS)
    k_rot = rotate(keys, positions, KVHEADS)
    group_size = QHEADS // KVHEADS
    scale = HEAD_DIM ** -0.5
    query_heads = jnp.transpose(q_rot.astype(jnp.float32).reshape(TOKENS, QHEADS, HEAD_DIM), (1, 0, 2))
    key_heads = jnp.transpose(k_rot.astype(jnp.float32).reshape(TOKENS, KVHEADS, HEAD_DIM), (1, 0, 2))
    value_heads = jnp.transpose(values.astype(jnp.float32).reshape(TOKENS, KVHEADS, HEAD_DIM), (1, 0, 2))
    block_rows = math.gcd(TOKENS, 1024)

    def per_head(head_index):
        query_head = query_heads[head_index]
        key_head = key_heads[head_index // group_size]
        value_head = value_heads[head_index // group_size]

        def per_block(start):
            rows_here = lax.dynamic_slice_in_dim(query_head, start, block_rows, 0)
            places_here = lax.dynamic_slice_in_dim(positions, start, block_rows, 0)
            scores = jnp.dot(rows_here, key_head.T, precision=lax.Precision.HIGHEST, preferred_element_type=jnp.float32) * scale
            visible = positions[None, :] <= places_here[:, None]
            highest = jnp.max(jnp.where(visible, scores, -jnp.inf), axis=1, keepdims=True)
            weights = jnp.where(visible, jnp.exp(scores - highest), 0.0)
            total = jnp.sum(weights, axis=1, keepdims=True)
            rounded = lax.optimization_barrier(weights.astype(jnp.bfloat16)).astype(jnp.float32)
            return jnp.dot(rounded, value_head, precision=lax.Precision.HIGHEST, preferred_element_type=jnp.float32) / total

        starts = jnp.arange(0, TOKENS, block_rows, dtype=jnp.int32)
        return lax.map(per_block, starts).reshape(TOKENS, HEAD_DIM)

    attended = lax.map(per_head, jnp.arange(QHEADS, dtype=jnp.int32))
    return jnp.transpose(attended, (1, 0, 2)).reshape(TOKENS, QHEADS * HEAD_DIM).astype(jnp.bfloat16)
```

```python
import functools
import math

import jax
import jax.numpy as jnp
import numpy as np
from jax import lax
from jax.experimental import pallas as pl
from jax.experimental.pallas import tpu as pltpu
from jax.sharding import PartitionSpec as P

QHEADS = 32
KVHEADS = 4
HEAD_DIM = 128


def rope_table(size):
    entries = []
    for number in range(size // 2):
        inverse = 1.0 / 500000.0 ** (2.0 * number / size)
        wavelength = 2.0 * math.pi / inverse
        if wavelength < 2048.0:
            entries.append(inverse)
        elif wavelength > 8192.0:
            entries.append(inverse / 8.0)
        else:
            smooth = (8192.0 / wavelength - 1.0) / 3.0
            entries.append((1.0 - smooth) * inverse / 8.0 + smooth * inverse)
    return np.array(entries, dtype=np.float32)


F32 = jnp.float32
BF16 = jnp.bfloat16
MESH = pl.DeviceIdType.MESH
SCALE = math.log2(math.e) * HEAD_DIM ** (-0.5)
SAFE = 100.0
NORM_CAP = (SAFE / SCALE) ** 2
PART = 64
SPAN = 128
GROUP = QHEADS // KVHEADS
COLS = GROUP * SPAN
EXTRA = 16
ROWS = 4 * SPAN + EXTRA
HALF = 256
PIECE = 2 * PART + EXTRA
NBLK = 8
CHUNK = 512
TAIL = 256


def turn(x, cosine, sine):
    return x * cosine + pltpu.roll(x, HEAD_DIM // 2, 1) * sine


def fused(
    shifted,
    q_hbm, k_hbm, v_hbm, pos_hbm, table_hbm,
    out_ref, ok_ref,
    q_ref, k_ref, v_ref, pos_ref, table_ref,
    kv, piece_out, piece_in, q_out, q_in, qc, ka, kc, va, vc, flags,
    acc_lo, acc_hi, top_lo, top_hi, o_out,
    in_sem, p_ss, p_rs, q_ss, q_rs, o_ss, o_rs, rs, rsc, ss_core, ss1, ss2, ss_z,
):
    blk = lax.axis_index("blk")
    hd = lax.axis_index("head")
    core = blk % 2
    zz = (blk // 2) % 2
    yy = (blk // 4) % 4
    xx = blk // 16

    def bid(x, y, z, c):
        return (((x + 8) % 4) * 4 + (y + 8) % 4) * 4 + z * 2 + c

    xp, xm = bid(xx + 1, yy, zz, core), bid(xx + 3, yy, zz, core)
    yp, ym = bid(xx, yy + 1, zz, core), bid(xx, yy + 3, zz, core)
    zn = bid(xx, yy, 1 - zz, core)
    cn = bid(xx, yy, zz, 1 - core)

    barrier = pltpu.get_barrier_semaphore()
    for peer in (xp, xm, yp, ym, zn, cn):
        pl.semaphore_signal(barrier, inc=1, device_id=(peer, hd), device_id_type=MESH)
    for d in (1, 2, 3):
        pl.semaphore_signal(barrier, inc=1, device_id=(blk, (hd + d) % 4), device_id_type=MESH)

    loads = [
        pltpu.make_async_copy(a, b, in_sem.at[n])
        for n, (a, b) in enumerate((
            (pos_hbm, pos_ref), (table_hbm, table_ref), (k_hbm, k_ref), (v_hbm, v_ref), (q_hbm, q_ref)))
    ]
    for load in loads:
        load.start()

    ones_m = jnp.ones((HEAD_DIM, HEAD_DIM), BF16)

    def norms(ref, count):
        best = jnp.zeros((PART, HEAD_DIM), F32)
        for g in range(count):
            x = ref[:, g * HEAD_DIM : (g + 1) * HEAD_DIM].astype(F32)
            best = jnp.maximum(best, jnp.dot((x * x).astype(BF16), ones_m, preferred_element_type=F32))
        return jnp.max(best, axis=0, keepdims=True) * 1.03

    row16 = lax.broadcasted_iota(jnp.int32, (EXTRA, HEAD_DIM), 0)

    def extras(span, qn, kn):
        return jnp.where(row16 < 4, span, jnp.where(row16 < 8, qn, kn)).astype(BF16)

    loads[0].wait()
    loads[1].wait()
    place = pos_ref[0]
    angles = (place + lax.broadcasted_iota(jnp.int32, (PART, HEAD_DIM), 0)).astype(F32) * table_ref[0:1]
    cosine = jnp.cos(angles)
    sine = jnp.sin(angles)
    sine = jnp.where(lax.broadcasted_iota(jnp.int32, (PART, HEAD_DIM), 1) < HEAD_DIM // 2, -sine, sine)
    for load in loads[2:]:
        load.wait()
    span = jnp.full((1, HEAD_DIM), place // SPAN, jnp.int32).astype(F32)
    ext = extras(span, norms(q_ref, QHEADS), norms(k_ref, KVHEADS))
    for g in range(KVHEADS):
        cols = slice(g * HEAD_DIM, (g + 1) * HEAD_DIM)
        piece_out[g, 0:PART] = turn(k_ref[:, cols].astype(F32), cosine, sine).astype(BF16)
        piece_out[g, PART : 2 * PART] = v_ref[:, cols]
        piece_out[g, 2 * PART : PIECE] = ext
    pl.semaphore_wait(barrier, 9)

    def piece_copy(d):
        tgt = (hd + d) % 4
        return pltpu.make_async_remote_copy(
            src_ref=piece_out.at[tgt], dst_ref=piece_in.at[hd],
            send_sem=p_ss.at[d - 1], recv_sem=p_rs.at[d - 1],
            device_id=(blk, tgt), device_id_type=MESH)

    for d in (2, 1, 3):
        piece_copy(d).start()
    piece_in[hd] = piece_out[hd]

    for g in range(KVHEADS):
        for i in range(GROUP):
            n = g * GROUP + i
            x = q_ref[:, n * HEAD_DIM : (n + 1) * HEAD_DIM].astype(F32)
            q_out[g, i * PART : (i + 1) * PART] = turn(x, cosine, sine).astype(BF16)

    def q_copy(d):
        tgt = (hd + d) % 4
        return pltpu.make_async_remote_copy(
            src_ref=q_out.at[tgt], dst_ref=q_in.at[hd],
            send_sem=q_ss.at[d - 1], recv_sem=q_rs.at[d - 1],
            device_id=(blk, tgt), device_id_type=MESH)

    def recv_piece(d):
        src = (hd + 4 - d) % 4
        pltpu.make_async_remote_copy(
            src_ref=piece_out.at[src], dst_ref=piece_in.at[src],
            send_sem=p_ss.at[d - 1], recv_sem=p_rs.at[d - 1],
            device_id=(blk, src), device_id_type=MESH).wait_recv()

    def recv_q(d):
        src = (hd + 4 - d) % 4
        pltpu.make_async_remote_copy(
            src_ref=q_out.at[src], dst_ref=q_in.at[src],
            send_sem=q_ss.at[d - 1], recv_sem=q_rs.at[d - 1],
            device_id=(blk, src), device_id_type=MESH).wait_recv()

    for d in (1, 2, 3):
        recv_piece(d)

    e = [piece_in[h, 2 * PART : PIECE].astype(F32) for h in range(4)]
    s0, s1 = e[0][0:1], e[2][0:1]
    low_first = s0 < s1
    mine = jnp.minimum(s0, s1)
    qn = jnp.maximum(jnp.maximum(e[0][4:5], e[1][4:5]), jnp.maximum(e[2][4:5], e[3][4:5]))
    kn = jnp.maximum(jnp.maximum(e[0][8:9], e[1][8:9]), jnp.maximum(e[2][8:9], e[3][8:9]))
    pick = jnp.broadcast_to(low_first, (SPAN, HEAD_DIM))

    def spans(load):
        first = jnp.concatenate([load(0), load(1)], axis=0).astype(F32)
        second = jnp.concatenate([load(2), load(3)], axis=0).astype(F32)
        return first, second

    k0, k1 = spans(lambda h: piece_in[h, 0:PART])
    v0, v1 = spans(lambda h: piece_in[h, PART : 2 * PART])
    v0, v1 = v0.T, v1.T
    kv[blk, 0:SPAN] = jnp.where(pick, k0, k1).astype(BF16)
    kv[blk, SPAN : 2 * SPAN] = jnp.where(pick, k1, k0).astype(BF16)
    kv[blk, 2 * SPAN : 3 * SPAN] = jnp.where(pick, v0, v1).astype(BF16)
    kv[blk, 3 * SPAN : 4 * SPAN] = jnp.where(pick, v1, v0).astype(BF16)
    kv[blk, 4 * SPAN : ROWS] = extras(mine, qn, kn)

    def slot(t, p, i, c):
        x = xx + (1 - t) * i + t * p
        y = yy + (1 - t) * p + t * i
        z = zz + t - 2 * zz * t
        return bid(x, y, z, c)

    def copy(t, p, i, lo, n, dev, ss, sem):
        b = slot(t, p, i, core)
        ref = kv.at[b, pl.ds(lo, n)]
        return pltpu.make_async_remote_copy(
            src_ref=ref, dst_ref=ref, send_sem=ss, recv_sem=sem,
            device_id=(dev, hd), device_id_type=MESH)

    def rid(t, p, i):
        return t * 16 + p * 4 + i

    def near(t, axis, d):
        a = t if axis == 0 else 1 - t
        return bid(xx + (1 - a) * d, yy + a * d, zz, core)

    def core_copy(t, p, i):
        return copy(t, p, i, 0, ROWS, cn, ss_core.at[rid(t, p, i)], rsc.at[rid(t, p, i)])

    def core_recv(t, p, i):
        b = slot(t, p, i, 1 - core)
        ref = kv.at[b]
        pltpu.make_async_remote_copy(
            src_ref=ref, dst_ref=ref, send_sem=ss_core.at[rid(t, p, i)],
            recv_sem=rsc.at[rid(t, p, i)], device_id=(cn, hd), device_id_type=MESH).wait_recv()

    def z_copy():
        return pltpu.make_async_remote_copy(
            src_ref=kv.at[blk], dst_ref=kv.at[blk], send_sem=ss_z.at[0],
            recv_sem=rs.at[rid(1, 0, 0), 0], device_id=(zn, hd), device_id_type=MESH)

    def first_copy(t, d):
        return copy(t, 0, 0, 0, ROWS, near(t, 0, d), ss1.at[t * 4 + (0 if d == 1 else 1)],
                    rs.at[rid(t, 0, 3 if d == 1 else 1), 0])

    def first_forward(t, d):
        lo, n = (0, HALF) if d == 1 else (HALF, ROWS - HALF)
        return copy(t, 0, 3 if d == 1 else 1, lo, n, near(t, 0, d),
                    ss1.at[t * 4 + (2 if d == 1 else 3)], rs.at[rid(t, 0, 2), 0 if d == 1 else 1])

    def second_copy(t, i, d):
        return copy(t, 0, i, 0, ROWS, near(t, 1, d), ss2.at[t * 16 + i * 4 + (0 if d == 1 else 1)],
                    rs.at[rid(t, 3 if d == 1 else 1, i), 0])

    def second_forward(t, i, d):
        lo, n = (0, HALF) if d == 1 else (HALF, ROWS - HALF)
        return copy(t, 3 if d == 1 else 1, i, lo, n, near(t, 1, d),
                    ss2.at[t * 16 + i * 4 + (2 if d == 1 else 3)],
                    rs.at[rid(t, 2, i), 0 if d == 1 else 1])

    def recv_full(t, p, i):
        copy(t, p, i, 0, ROWS, cn, ss_core.at[rid(t, p, i)], rs.at[rid(t, p, i), 0]).wait_recv()

    def recv_halves(t, p, i):
        for part, (lo, n) in enumerate(((0, HALF), (HALF, ROWS - HALF))):
            copy(t, p, i, lo, n, cn, ss_core.at[rid(t, p, i)], rs.at[rid(t, p, i), part]).wait_recv()

    def second(t, i):
        for d in (1, -1):
            second_copy(t, i, d).start()

    def arrive(t, p, i):
        if p == 2:
            recv_halves(t, p, i)
        else:
            recv_full(t, p, i)
            second_forward(t, i, 1 if p == 3 else -1).start()
        core_copy(t, p, i).start()

    def spread(t, i):
        second(t, i)
        core_copy(t, 0, i).start()

    z_copy().start()
    for d in (1, -1):
        first_copy(0, d).start()
    spread(0, 0)
    recv_full(1, 0, 0)
    for d in (1, -1):
        first_copy(1, d).start()
    spread(1, 0)
    for d in (2, 1, 3):
        q_copy(d).start()
    q_in[hd] = q_out[hd]
    for t in (0, 1):
        for d in (1, -1):
            recv_full(t, 0, 3 if d == 1 else 1)
            first_forward(t, d).start()
            spread(t, 3 if d == 1 else 1)
    for t in (0, 1):
        recv_halves(t, 0, 2)
        spread(t, 2)

    acc_lo[...] = jnp.zeros_like(acc_lo)
    acc_hi[...] = jnp.zeros_like(acc_hi)
    for s in range(2):
        va[s, SPAN : SPAN + EXTRA] = jnp.ones((EXTRA, NBLK * SPAN), BF16)

    def prepare_queries():
        for d in (1, 2, 3):
            recv_q(d)
        for i in range(GROUP):
            a, b = spans(lambda h: q_in[h, i * PART : (i + 1) * PART])
            a, b = a.T, b.T
            qc[0:SPAN, i * SPAN : (i + 1) * SPAN] = jnp.where(pick, a, b).astype(BF16)
            qc[SPAN:, i * SPAN : (i + 1) * SPAN] = jnp.where(pick, b, a).astype(BF16)

    def diagonal():
        key_row = lax.broadcasted_iota(jnp.int32, (SPAN, COLS), 0)
        token = lax.broadcasted_iota(jnp.int32, (SPAN, COLS), 1) % SPAN
        seen = key_row <= token
        for n, (acc, top) in enumerate(((acc_lo, top_lo), (acc_hi, top_hi))):
            keys = kv[blk, n * SPAN : (n + 1) * SPAN]
            vals = kv[blk, (2 + n) * SPAN : (3 + n) * SPAN]
            scores = jnp.dot(keys, qc[n * SPAN : (n + 1) * SPAN], preferred_element_type=F32) * SCALE
            if shifted:
                best = jnp.max(jnp.where(seen, scores, -1e30), axis=0, keepdims=True)
                top[...] = jnp.broadcast_to(best, (8, COLS))
                scores = scores - best
            weights = jnp.where(seen, jnp.exp2(scores), 0.0).astype(BF16)
            vals = jnp.concatenate([vals, jnp.ones((EXTRA, SPAN), BF16)], axis=0)
            acc[...] += jnp.dot(vals, weights, preferred_element_type=F32)[0 : SPAN + 8]

    def gather_stage(t, p, s):
        for i in range(4):
            core_recv(t, p, i)
        for c in range(2):
            for i in range(4):
                n = c * 4 + i
                keys = slice(n * SPAN, (n + 1) * SPAN)
                b = slot(t, p, i, core if c == 0 else 1 - core)
                j = kv[b, 4 * SPAN : ROWS].astype(F32)[0:1]
                below = jnp.where(j < mine, 1.0, 0.0)
                above = jnp.where(j > mine, 1.0, 0.0)
                lower = jnp.broadcast_to(below, (SPAN, HEAD_DIM)).astype(BF16)
                upper = jnp.broadcast_to(above, (SPAN, HEAD_DIM)).astype(BF16)
                k_low = kv[b, 0:SPAN]
                v_low = kv[b, 2 * SPAN : 3 * SPAN]
                ka[s, keys] = k_low
                va[s, 0:SPAN, keys] = v_low
                kc[s, keys, 0:SPAN] = k_low * lower
                kc[s, keys, SPAN:] = kv[b, SPAN : 2 * SPAN] * upper
                vc[s, 0:SPAN, keys] = v_low * lower
                vc[s, SPAN : 2 * SPAN, keys] = kv[b, 3 * SPAN : 4 * SPAN] * upper
                vc[s, 2 * SPAN :, keys] = jnp.where(row16 < 8, below, above).astype(BF16)
                if shifted:
                    flags[s, n] = jnp.where(row16 < 8, below, above)

    def add_both(both, cols, scale_lo, scale_hi):
        acc_lo[0:SPAN, cols] = acc_lo[0:SPAN, cols] * scale_lo + both[0:SPAN]
        acc_lo[SPAN:, cols] = acc_lo[SPAN:, cols] * scale_lo + both[2 * SPAN : 2 * SPAN + 8]
        acc_hi[0:SPAN, cols] = acc_hi[0:SPAN, cols] * scale_hi + both[SPAN : 2 * SPAN]
        acc_hi[SPAN:, cols] = acc_hi[SPAN:, cols] * scale_hi + both[2 * SPAN + 8 :]

    def work_shifted(s, cols):
        width = cols.stop - cols.start

        @pl.loop(0, NBLK)
        def _(n):
            keys = pl.ds(pl.multiple_of(n * SPAN, SPAN), SPAN)
            lower = jnp.concatenate([flags[s, n, 0:1]] * (width // HEAD_DIM), axis=1) > 0.5
            upper = jnp.concatenate([flags[s, n, 8:9]] * (width // HEAD_DIM), axis=1) > 0.5
            scores = jnp.dot(ka[s, keys], qc[SPAN:, cols], preferred_element_type=F32) * SCALE
            old = top_hi[0:1, cols]
            new = jnp.maximum(old, jnp.max(scores, axis=0, keepdims=True))
            weights = jnp.exp2(scores - new).astype(BF16)
            part = jnp.dot(va[s, :, keys], weights, preferred_element_type=F32)[0 : SPAN + 8]
            acc_hi[:, cols] = acc_hi[:, cols] * jnp.exp2(old - new) + part
            old_hi, old_lo = new, top_lo[0:1, cols]
            scores = jnp.dot(kc[s, keys], qc[:, cols], preferred_element_type=F32) * SCALE
            best = jnp.max(scores, axis=0, keepdims=True)
            new_lo = jnp.where(lower, jnp.maximum(old_lo, best), old_lo)
            new_hi = jnp.where(upper, jnp.maximum(old_hi, best), old_hi)
            shift = jnp.where(lower, new_lo, new_hi)
            weights = jnp.where(lower | upper, jnp.exp2(scores - shift), 0.0).astype(BF16)
            both = jnp.dot(vc[s, :, keys], weights, preferred_element_type=F32)
            add_both(both, cols, jnp.exp2(old_lo - new_lo), jnp.exp2(old_hi - new_hi))
            top_lo[:, cols] = jnp.broadcast_to(new_lo, (8, width))
            top_hi[:, cols] = jnp.broadcast_to(new_hi, (8, width))

    def work(s, cols):
        if shifted:
            work_shifted(s, cols)
            return
        scores = jnp.dot(ka[s], qc[SPAN:, cols], preferred_element_type=F32)
        weights = jnp.exp2(scores * SCALE).astype(BF16)
        acc_hi[:, cols] += jnp.dot(va[s], weights, preferred_element_type=F32)[0 : SPAN + 8]
        scores = jnp.dot(kc[s], qc[:, cols], preferred_element_type=F32)
        weights = jnp.exp2(scores * SCALE).astype(BF16)
        both = jnp.dot(vc[s], weights, preferred_element_type=F32)
        acc_lo[0:SPAN, cols] += both[0:SPAN]
        acc_lo[SPAN:, cols] += both[2 * SPAN : 2 * SPAN + 8]
        acc_hi[0:SPAN, cols] += both[SPAN : 2 * SPAN]
        acc_hi[SPAN:, cols] += both[2 * SPAN + 8 :]

    halves = [slice(c * CHUNK, (c + 1) * CHUNK) for c in range(COLS // CHUNK)]
    tails = [slice(c * TAIL, (c + 1) * TAIL) for c in range(COLS // TAIL)]

    def stage(t, p, s, between=()):
        gather_stage(t, p, s)
        between = list(between)
        for n, cols in enumerate(halves):
            work(s, cols)
            share = -(-len(between) // (len(halves) - n))
            for task in between[:share]:
                arrive(*task)
            between = between[share:]

    def o_copy(d, c, src):
        tgt = (hd + d) % 4
        start = pl.multiple_of(src * COLS + c * TAIL, TAIL)
        return pltpu.make_async_remote_copy(
            src_ref=o_out.at[tgt, :, pl.ds(c * TAIL, TAIL)], dst_ref=out_ref.at[:, pl.ds(start, TAIL)],
            send_sem=o_ss.at[d - 1, c], recv_sem=o_rs.at[d - 1, c],
            device_id=(blk, tgt), device_id_type=MESH)

    def own_copy(c):
        start = pl.multiple_of(hd * COLS + c * TAIL, TAIL)
        return pltpu.make_async_copy(
            o_out.at[hd, :, pl.ds(c * TAIL, TAIL)], out_ref.at[:, pl.ds(start, TAIL)], o_ss.at[3, c])

    def finish(c):
        for i in range(c * TAIL // SPAN, (c + 1) * TAIL // SPAN):
            cols = slice(i * SPAN, (i + 1) * SPAN)
            low = (acc_lo[0:SPAN, cols] * (1.0 / acc_lo[SPAN : SPAN + 1, cols])).T
            high = (acc_hi[0:SPAN, cols] * (1.0 / acc_hi[SPAN : SPAN + 1, cols])).T
            first = jnp.where(pick, low, high).astype(BF16)
            second_rows = jnp.where(pick, high, low).astype(BF16)
            o_out[0, :, cols] = first[:PART]
            o_out[1, :, cols] = first[PART:]
            o_out[2, :, cols] = second_rows[:PART]
            o_out[3, :, cols] = second_rows[PART:]
        for d in (2, 1, 3):
            o_copy(d, c, hd).start()
        own_copy(c).start()

    def ring(t, p):
        return [(t, p, i) for i in (0, 3, 1, 2)]

    def take(tasks):
        for task in tasks:
            arrive(*task)

    prepare_queries()
    diagonal()
    stage(0, 0, 0)
    take(ring(0, 3) + ring(0, 1) + ring(1, 3) + ring(1, 1))
    stage(1, 0, 1)
    stage(0, 3, 0)
    stage(1, 3, 1)
    take(ring(0, 2) + ring(1, 2))
    stage(0, 1, 0)
    stage(1, 1, 1)
    gather_stage(0, 2, 0)
    gather_stage(1, 2, 1)
    for c, cols in enumerate(tails):
        work(0, cols)
        work(1, cols)
        finish(c)
    def worst(b, carry):
        x = kv[b, 4 * SPAN : ROWS].astype(F32)
        return jnp.maximum(carry, x)

    top = lax.fori_loop(0, 64, worst, jnp.zeros((EXTRA, HEAD_DIM), F32))
    ok_ref[0, 0] = jnp.max(jnp.where(top[4:5] * top[8:9] <= NORM_CAP, 1, 0))

    for d in (1, 2, 3):
        piece_copy(d).wait_send()
        q_copy(d).wait_send()
    z_copy().wait_send()
    for t in (0, 1):
        for d in (1, -1):
            first_copy(t, d).wait_send()
            first_forward(t, d).wait_send()

        @pl.loop(0, 4)
        def _(i):
            for d in (1, -1):
                second_copy(t, i, d).wait_send()
                second_forward(t, i, d).wait_send()
            for p in range(4):
                core_copy(t, p, i).wait_send()
    for c in range(len(tails)):
        own_copy(c).wait()
        for d in (1, 2, 3):
            o_copy(d, c, hd).wait_send()
            o_copy(d, c, (hd + 4 - d) % 4).wait_recv()


def attention(shifted, queries, keys, values, positions):
    vmem = pl.BlockSpec(memory_space=pltpu.VMEM)
    anywhere = pl.BlockSpec(memory_space=pl.ANY)
    dma = pltpu.SemaphoreType.DMA
    wide = NBLK * SPAN
    table = rope_table(HEAD_DIM)
    table = jnp.asarray(np.tile(np.concatenate([table, table])[None], (8, 1)))
    return pl.pallas_call(
        functools.partial(fused, shifted),
        out_shape=(
            jax.ShapeDtypeStruct((PART, QHEADS * HEAD_DIM), BF16),
            jax.ShapeDtypeStruct((1, 1), jnp.int32),
        ),
        in_specs=[anywhere] * 5,
        out_specs=(anywhere, pl.BlockSpec(memory_space=pltpu.SMEM)),
        scratch_shapes=[
            pltpu.VMEM((PART, QHEADS * HEAD_DIM), BF16),
            pltpu.VMEM((PART, KVHEADS * HEAD_DIM), BF16),
            pltpu.VMEM((PART, KVHEADS * HEAD_DIM), BF16),
            pltpu.SMEM((PART,), jnp.int32),
            pltpu.VMEM((8, HEAD_DIM), F32),
            pltpu.VMEM((64, ROWS, HEAD_DIM), BF16),
            pltpu.VMEM((4, PIECE, HEAD_DIM), BF16),
            pltpu.VMEM((4, PIECE, HEAD_DIM), BF16),
            pltpu.VMEM((4, GROUP * PART, HEAD_DIM), BF16),
            pltpu.VMEM((4, GROUP * PART, HEAD_DIM), BF16),
            pltpu.VMEM((2 * HEAD_DIM, COLS), BF16),
            pltpu.VMEM((2, wide, HEAD_DIM), BF16),
            pltpu.VMEM((2, wide, 2 * HEAD_DIM), BF16),
            pltpu.VMEM((2, SPAN + EXTRA, wide), BF16),
            pltpu.VMEM((2, 2 * SPAN + EXTRA, wide), BF16),
            pltpu.VMEM((2, NBLK, EXTRA, HEAD_DIM), F32),
            pltpu.VMEM((SPAN + 8, COLS), F32),
            pltpu.VMEM((SPAN + 8, COLS), F32),
            pltpu.VMEM((8, COLS), F32),
            pltpu.VMEM((8, COLS), F32),
            pltpu.VMEM((4, PART, COLS), BF16),
            dma((5,)), dma((3,)), dma((3,)), dma((3,)), dma((3,)),
            dma((4, COLS // TAIL)), dma((3, COLS // TAIL)),
            dma((32, 2)), dma((32,)), dma((32,)), dma((8,)), dma((32,)), dma((1,)),
        ],
        compiler_params=pltpu.CompilerParams(
            collective_id=int(shifted), has_side_effects=True, vmem_limit_bytes=48 * 1024 * 1024
        ),
    )(queries, keys, values, positions, table)


def body(queries, keys, values, positions):
    quick, fine = attention(False, queries, keys, values, positions)
    return lax.cond(
        fine[0, 0] == 1,
        lambda: quick,
        lambda: attention(True, queries, keys, values, positions)[0],
    )


def solution(mesh):
    return jax.shard_map(
        body,
        mesh=mesh,
        in_specs=(
            P(("blk", "head"), None),
            P(("blk", "head"), None),
            P(("blk", "head"), None),
            P(("blk", "head")),
        ),
        out_specs=P(("blk", "head"), None),
        check_vma=False,
    )
```

```python
import functools
import math

import jax
import jax.numpy as jnp
import numpy as np
from jax import lax
from jax.experimental import pallas as pl
from jax.experimental.pallas import tpu as pltpu
from jax.sharding import PartitionSpec as P

QHEADS = 32
KVHEADS = 4
HEAD_DIM = 128


def rope_table(size):
    entries = []
    for number in range(size // 2):
        inverse = 1.0 / 500000.0 ** (2.0 * number / size)
        wavelength = 2.0 * math.pi / inverse
        if wavelength < 2048.0:
            entries.append(inverse)
        elif wavelength > 8192.0:
            entries.append(inverse / 8.0)
        else:
            smooth = (8192.0 / wavelength - 1.0) / 3.0
            entries.append((1.0 - smooth) * inverse / 8.0 + smooth * inverse)
    return np.array(entries, dtype=np.float32)


F32 = jnp.float32
BF16 = jnp.bfloat16
MESH = pl.DeviceIdType.MESH
SCALE = math.log2(math.e) * HEAD_DIM ** (-0.5)
SAFE = 100.0
NORM_CAP = (SAFE / SCALE) ** 2
PART = 64
SPAN = 128
GROUP = QHEADS // KVHEADS
COLS = GROUP * SPAN
EXTRA = 16
ROWS = 4 * SPAN + EXTRA
HALF = 256
PIECE = 2 * PART + EXTRA
NBLK = 8
CHUNK = 512
TAIL = 256


def turn(x, cosine, sine):
    return x * cosine + pltpu.roll(x, HEAD_DIM // 2, 1) * sine


def fused(
    shifted,
    q_hbm, k_hbm, v_hbm, pos_hbm, table_hbm,
    out_ref, ok_ref,
    q_ref, k_ref, v_ref, pos_ref, table_ref,
    kv, piece_out, piece_in, layer_in, q_out, q_in, qc, ka, kc, va, vc, flags,
    acc_lo, acc_hi, top_lo, top_hi, o_out,
    in_sem, p_ss, p_rs, q_ss, q_rs, o_ss, o_rs, rs, rsc, ss_core, ss1, ss2, l_ss, l_rs,
):
    blk = lax.axis_index("blk")
    hd = lax.axis_index("head")
    core = blk % 2
    zz = (blk // 2) % 2
    yy = (blk // 4) % 4
    xx = blk // 16

    def bid(x, y, z, c):
        return (((x + 8) % 4) * 4 + (y + 8) % 4) * 4 + z * 2 + c

    xp, xm = bid(xx + 1, yy, zz, core), bid(xx + 3, yy, zz, core)
    yp, ym = bid(xx, yy + 1, zz, core), bid(xx, yy + 3, zz, core)
    zn = bid(xx, yy, 1 - zz, core)
    cn = bid(xx, yy, zz, 1 - core)

    barrier = pltpu.get_barrier_semaphore()
    for peer in (xp, xm, yp, ym, zn, cn):
        pl.semaphore_signal(barrier, inc=1, device_id=(peer, hd), device_id_type=MESH)
    for d in (1, 2, 3):
        pl.semaphore_signal(barrier, inc=1, device_id=(blk, (hd + d) % 4), device_id_type=MESH)
        pl.semaphore_signal(barrier, inc=1, device_id=(zn, (hd + d) % 4), device_id_type=MESH)

    loads = [
        pltpu.make_async_copy(a, b, in_sem.at[n])
        for n, (a, b) in enumerate((
            (pos_hbm, pos_ref), (table_hbm, table_ref), (k_hbm, k_ref), (v_hbm, v_ref), (q_hbm, q_ref)))
    ]
    for load in loads:
        load.start()

    ones_m = jnp.ones((HEAD_DIM, HEAD_DIM), BF16)

    def norms(ref, count):
        best = jnp.zeros((PART, HEAD_DIM), F32)
        for g in range(count):
            x = ref[:, g * HEAD_DIM : (g + 1) * HEAD_DIM].astype(F32)
            best = jnp.maximum(best, jnp.dot((x * x).astype(BF16), ones_m, preferred_element_type=F32))
        return jnp.max(best, axis=0, keepdims=True) * 1.03

    row16 = lax.broadcasted_iota(jnp.int32, (EXTRA, HEAD_DIM), 0)

    def extras(span, qn, kn):
        return jnp.where(row16 < 4, span, jnp.where(row16 < 8, qn, kn)).astype(BF16)

    loads[0].wait()
    loads[1].wait()
    place = pos_ref[0]
    angles = (place + lax.broadcasted_iota(jnp.int32, (PART, HEAD_DIM), 0)).astype(F32) * table_ref[0:1]
    cosine = jnp.cos(angles)
    sine = jnp.sin(angles)
    sine = jnp.where(lax.broadcasted_iota(jnp.int32, (PART, HEAD_DIM), 1) < HEAD_DIM // 2, -sine, sine)
    for load in loads[2:]:
        load.wait()
    span = jnp.full((1, HEAD_DIM), place // SPAN, jnp.int32).astype(F32)
    ext = extras(span, norms(q_ref, QHEADS), norms(k_ref, KVHEADS))
    for g in range(KVHEADS):
        cols = slice(g * HEAD_DIM, (g + 1) * HEAD_DIM)
        piece_out[g, 0:PART] = turn(k_ref[:, cols].astype(F32), cosine, sine).astype(BF16)
        piece_out[g, PART : 2 * PART] = v_ref[:, cols]
        piece_out[g, 2 * PART : PIECE] = ext
    pl.semaphore_wait(barrier, 12)

    def piece_copy(d):
        tgt = (hd + d) % 4
        return pltpu.make_async_remote_copy(
            src_ref=piece_out.at[tgt], dst_ref=piece_in.at[hd],
            send_sem=p_ss.at[d - 1], recv_sem=p_rs.at[d - 1],
            device_id=(blk, tgt), device_id_type=MESH)

    def layer_copy(d):
        tgt = (hd + d) % 4
        return pltpu.make_async_remote_copy(
            src_ref=piece_out.at[tgt], dst_ref=layer_in.at[hd],
            send_sem=l_ss.at[d], recv_sem=l_rs.at[d],
            device_id=(zn, tgt), device_id_type=MESH)

    def recv_layer(d):
        src = (hd + 4 - d) % 4
        pltpu.make_async_remote_copy(
            src_ref=piece_out.at[src], dst_ref=layer_in.at[src],
            send_sem=l_ss.at[d], recv_sem=l_rs.at[d],
            device_id=(zn, src), device_id_type=MESH).wait_recv()

    for d in (2, 1, 3):
        piece_copy(d).start()
    for d in (2, 1, 3, 0):
        layer_copy(d).start()
    piece_in[hd] = piece_out[hd]

    for g in range(KVHEADS):
        for i in range(GROUP):
            n = g * GROUP + i
            x = q_ref[:, n * HEAD_DIM : (n + 1) * HEAD_DIM].astype(F32)
            q_out[g, i * PART : (i + 1) * PART] = turn(x, cosine, sine).astype(BF16)

    def q_copy(d):
        tgt = (hd + d) % 4
        return pltpu.make_async_remote_copy(
            src_ref=q_out.at[tgt], dst_ref=q_in.at[hd],
            send_sem=q_ss.at[d - 1], recv_sem=q_rs.at[d - 1],
            device_id=(blk, tgt), device_id_type=MESH)

    def recv_piece(d):
        src = (hd + 4 - d) % 4
        pltpu.make_async_remote_copy(
            src_ref=piece_out.at[src], dst_ref=piece_in.at[src],
            send_sem=p_ss.at[d - 1], recv_sem=p_rs.at[d - 1],
            device_id=(blk, src), device_id_type=MESH).wait_recv()

    def recv_q(d):
        src = (hd + 4 - d) % 4
        pltpu.make_async_remote_copy(
            src_ref=q_out.at[src], dst_ref=q_in.at[src],
            send_sem=q_ss.at[d - 1], recv_sem=q_rs.at[d - 1],
            device_id=(blk, src), device_id_type=MESH).wait_recv()

    for d in (1, 2, 3):
        recv_piece(d)

    def spans(load):
        first = jnp.concatenate([load(0), load(1)], axis=0).astype(F32)
        second = jnp.concatenate([load(2), load(3)], axis=0).astype(F32)
        return first, second

    def assemble(pieces, b):
        e = [pieces[h, 2 * PART : PIECE].astype(F32) for h in range(4)]
        s0, s1 = e[0][0:1], e[2][0:1]
        least = jnp.minimum(s0, s1)
        qn = jnp.maximum(jnp.maximum(e[0][4:5], e[1][4:5]), jnp.maximum(e[2][4:5], e[3][4:5]))
        kn = jnp.maximum(jnp.maximum(e[0][8:9], e[1][8:9]), jnp.maximum(e[2][8:9], e[3][8:9]))
        low_first = jnp.broadcast_to(s0 < s1, (SPAN, HEAD_DIM))
        k0, k1 = spans(lambda h: pieces[h, 0:PART])
        v0, v1 = spans(lambda h: pieces[h, PART : 2 * PART])
        v0, v1 = v0.T, v1.T
        kv[b, 0:SPAN] = jnp.where(low_first, k0, k1).astype(BF16)
        kv[b, SPAN : 2 * SPAN] = jnp.where(low_first, k1, k0).astype(BF16)
        kv[b, 2 * SPAN : 3 * SPAN] = jnp.where(low_first, v0, v1).astype(BF16)
        kv[b, 3 * SPAN : 4 * SPAN] = jnp.where(low_first, v1, v0).astype(BF16)
        kv[b, 4 * SPAN : ROWS] = extras(least, qn, kn)
        return least, low_first

    mine, pick = assemble(piece_in, blk)

    def slot(t, p, i, c):
        x = xx + (1 - t) * i + t * p
        y = yy + (1 - t) * p + t * i
        z = zz + t - 2 * zz * t
        return bid(x, y, z, c)

    def copy(t, p, i, lo, n, dev, ss, sem):
        b = slot(t, p, i, core)
        ref = kv.at[b, pl.ds(lo, n)]
        return pltpu.make_async_remote_copy(
            src_ref=ref, dst_ref=ref, send_sem=ss, recv_sem=sem,
            device_id=(dev, hd), device_id_type=MESH)

    def rid(t, p, i):
        return t * 16 + p * 4 + i

    def near(t, axis, d):
        a = t if axis == 0 else 1 - t
        return bid(xx + (1 - a) * d, yy + a * d, zz, core)

    def core_copy(t, p, i):
        return copy(t, p, i, 0, ROWS, cn, ss_core.at[rid(t, p, i)], rsc.at[rid(t, p, i)])

    def core_recv(t, p, i):
        b = slot(t, p, i, 1 - core)
        ref = kv.at[b]
        pltpu.make_async_remote_copy(
            src_ref=ref, dst_ref=ref, send_sem=ss_core.at[rid(t, p, i)],
            recv_sem=rsc.at[rid(t, p, i)], device_id=(cn, hd), device_id_type=MESH).wait_recv()

    def first_copy(t, d):
        return copy(t, 0, 0, 0, ROWS, near(t, 0, d), ss1.at[t * 4 + (0 if d == 1 else 1)],
                    rs.at[rid(t, 0, 3 if d == 1 else 1), 0])

    def first_forward(t, d):
        lo, n = (0, HALF) if d == 1 else (HALF, ROWS - HALF)
        return copy(t, 0, 3 if d == 1 else 1, lo, n, near(t, 0, d),
                    ss1.at[t * 4 + (2 if d == 1 else 3)], rs.at[rid(t, 0, 2), 0 if d == 1 else 1])

    def second_copy(t, i, d):
        return copy(t, 0, i, 0, ROWS, near(t, 1, d), ss2.at[t * 16 + i * 4 + (0 if d == 1 else 1)],
                    rs.at[rid(t, 3 if d == 1 else 1, i), 0])

    def second_forward(t, i, d):
        lo, n = (0, HALF) if d == 1 else (HALF, ROWS - HALF)
        return copy(t, 3 if d == 1 else 1, i, lo, n, near(t, 1, d),
                    ss2.at[t * 16 + i * 4 + (2 if d == 1 else 3)],
                    rs.at[rid(t, 2, i), 0 if d == 1 else 1])

    def recv_full(t, p, i):
        copy(t, p, i, 0, ROWS, cn, ss_core.at[rid(t, p, i)], rs.at[rid(t, p, i), 0]).wait_recv()

    def recv_halves(t, p, i):
        for part, (lo, n) in enumerate(((0, HALF), (HALF, ROWS - HALF))):
            copy(t, p, i, lo, n, cn, ss_core.at[rid(t, p, i)], rs.at[rid(t, p, i), part]).wait_recv()

    def second(t, i):
        for d in (1, -1):
            second_copy(t, i, d).start()

    def arrive(t, p, i):
        if p == 2:
            recv_halves(t, p, i)
        else:
            recv_full(t, p, i)
            second_forward(t, i, 1 if p == 3 else -1).start()
        core_copy(t, p, i).start()

    for d in (1, -1):
        first_copy(0, d).start()
    for d in range(4):
        recv_layer(d)
    assemble(layer_in, zn)
    for d in (1, -1):
        first_copy(1, d).start()
    for t in (0, 1):
        second(t, 0)
        core_copy(t, 0, 0).start()
    for d in (2, 1, 3):
        q_copy(d).start()
    q_in[hd] = q_out[hd]
    for t in (0, 1):
        for d in (1, -1):
            i = 3 if d == 1 else 1
            recv_full(t, 0, i)
            first_forward(t, d).start()
            core_copy(t, 0, i).start()
    for i in (3, 1):
        for t in (0, 1):
            second(t, i)
    for t in (0, 1):
        recv_halves(t, 0, 2)
        second(t, 2)
        core_copy(t, 0, 2).start()

    acc_lo[...] = jnp.zeros_like(acc_lo)
    acc_hi[...] = jnp.zeros_like(acc_hi)
    for s in range(2):
        va[s, SPAN : SPAN + EXTRA] = jnp.ones((EXTRA, NBLK * SPAN), BF16)

    def prepare_queries():
        for d in (1, 2, 3):
            recv_q(d)
        for i in range(GROUP):
            a, b = spans(lambda h: q_in[h, i * PART : (i + 1) * PART])
            a, b = a.T, b.T
            qc[0:SPAN, i * SPAN : (i + 1) * SPAN] = jnp.where(pick, a, b).astype(BF16)
            qc[SPAN:, i * SPAN : (i + 1) * SPAN] = jnp.where(pick, b, a).astype(BF16)

    def diagonal():
        key_row = lax.broadcasted_iota(jnp.int32, (SPAN, COLS), 0)
        token = lax.broadcasted_iota(jnp.int32, (SPAN, COLS), 1) % SPAN
        seen = key_row <= token
        for n, (acc, top) in enumerate(((acc_lo, top_lo), (acc_hi, top_hi))):
            keys = kv[blk, n * SPAN : (n + 1) * SPAN]
            vals = kv[blk, (2 + n) * SPAN : (3 + n) * SPAN]
            scores = jnp.dot(keys, qc[n * SPAN : (n + 1) * SPAN], preferred_element_type=F32) * SCALE
            if shifted:
                best = jnp.max(jnp.where(seen, scores, -1e30), axis=0, keepdims=True)
                top[...] = jnp.broadcast_to(best, (8, COLS))
                scores = scores - best
            weights = jnp.where(seen, jnp.exp2(scores), 0.0).astype(BF16)
            vals = jnp.concatenate([vals, jnp.ones((EXTRA, SPAN), BF16)], axis=0)
            acc[...] += jnp.dot(vals, weights, preferred_element_type=F32)[0 : SPAN + 8]

    def gather_stage(t, p, s):
        for i in range(4):
            core_recv(t, p, i)
        for c in range(2):
            for i in range(4):
                n = c * 4 + i
                keys = slice(n * SPAN, (n + 1) * SPAN)
                b = slot(t, p, i, core if c == 0 else 1 - core)
                j = kv[b, 4 * SPAN : ROWS].astype(F32)[0:1]
                below = jnp.where(j < mine, 1.0, 0.0)
                above = jnp.where(j > mine, 1.0, 0.0)
                lower = jnp.broadcast_to(below, (SPAN, HEAD_DIM)).astype(BF16)
                upper = jnp.broadcast_to(above, (SPAN, HEAD_DIM)).astype(BF16)
                k_low = kv[b, 0:SPAN]
                v_low = kv[b, 2 * SPAN : 3 * SPAN]
                ka[s, keys] = k_low
                va[s, 0:SPAN, keys] = v_low
                kc[s, keys, 0:SPAN] = k_low * lower
                kc[s, keys, SPAN:] = kv[b, SPAN : 2 * SPAN] * upper
                vc[s, 0:SPAN, keys] = v_low * lower
                vc[s, SPAN : 2 * SPAN, keys] = kv[b, 3 * SPAN : 4 * SPAN] * upper
                vc[s, 2 * SPAN :, keys] = jnp.where(row16 < 8, below, above).astype(BF16)
                if shifted:
                    flags[s, n] = jnp.where(row16 < 8, below, above)

    def add_both(both, cols, scale_lo, scale_hi):
        acc_lo[0:SPAN, cols] = acc_lo[0:SPAN, cols] * scale_lo + both[0:SPAN]
        acc_lo[SPAN:, cols] = acc_lo[SPAN:, cols] * scale_lo + both[2 * SPAN : 2 * SPAN + 8]
        acc_hi[0:SPAN, cols] = acc_hi[0:SPAN, cols] * scale_hi + both[SPAN : 2 * SPAN]
        acc_hi[SPAN:, cols] = acc_hi[SPAN:, cols] * scale_hi + both[2 * SPAN + 8 :]

    def work_shifted(s, cols):
        width = cols.stop - cols.start

        @pl.loop(0, NBLK)
        def _(n):
            keys = pl.ds(pl.multiple_of(n * SPAN, SPAN), SPAN)
            lower = jnp.concatenate([flags[s, n, 0:1]] * (width // HEAD_DIM), axis=1) > 0.5
            upper = jnp.concatenate([flags[s, n, 8:9]] * (width // HEAD_DIM), axis=1) > 0.5
            scores = jnp.dot(ka[s, keys], qc[SPAN:, cols], preferred_element_type=F32) * SCALE
            old = top_hi[0:1, cols]
            new = jnp.maximum(old, jnp.max(scores, axis=0, keepdims=True))
            weights = jnp.exp2(scores - new).astype(BF16)
            part = jnp.dot(va[s, :, keys], weights, preferred_element_type=F32)[0 : SPAN + 8]
            acc_hi[:, cols] = acc_hi[:, cols] * jnp.exp2(old - new) + part
            old_hi, old_lo = new, top_lo[0:1, cols]
            scores = jnp.dot(kc[s, keys], qc[:, cols], preferred_element_type=F32) * SCALE
            best = jnp.max(scores, axis=0, keepdims=True)
            new_lo = jnp.where(lower, jnp.maximum(old_lo, best), old_lo)
            new_hi = jnp.where(upper, jnp.maximum(old_hi, best), old_hi)
            shift = jnp.where(lower, new_lo, new_hi)
            weights = jnp.where(lower | upper, jnp.exp2(scores - shift), 0.0).astype(BF16)
            both = jnp.dot(vc[s, :, keys], weights, preferred_element_type=F32)
            add_both(both, cols, jnp.exp2(old_lo - new_lo), jnp.exp2(old_hi - new_hi))
            top_lo[:, cols] = jnp.broadcast_to(new_lo, (8, width))
            top_hi[:, cols] = jnp.broadcast_to(new_hi, (8, width))

    def work(s, cols):
        if shifted:
            work_shifted(s, cols)
            return
        scores = jnp.dot(ka[s], qc[SPAN:, cols], preferred_element_type=F32)
        weights = jnp.exp2(scores * SCALE).astype(BF16)
        acc_hi[:, cols] += jnp.dot(va[s], weights, preferred_element_type=F32)[0 : SPAN + 8]
        scores = jnp.dot(kc[s], qc[:, cols], preferred_element_type=F32)
        weights = jnp.exp2(scores * SCALE).astype(BF16)
        both = jnp.dot(vc[s], weights, preferred_element_type=F32)
        acc_lo[0:SPAN, cols] += both[0:SPAN]
        acc_lo[SPAN:, cols] += both[2 * SPAN : 2 * SPAN + 8]
        acc_hi[0:SPAN, cols] += both[SPAN : 2 * SPAN]
        acc_hi[SPAN:, cols] += both[2 * SPAN + 8 :]

    halves = [slice(c * CHUNK, (c + 1) * CHUNK) for c in range(COLS // CHUNK)]
    tails = [slice(c * TAIL, (c + 1) * TAIL) for c in range(COLS // TAIL)]

    def stage(t, p, s, between=()):
        gather_stage(t, p, s)
        between = list(between)
        for n, cols in enumerate(halves):
            work(s, cols)
            share = -(-len(between) // (len(halves) - n))
            for task in between[:share]:
                arrive(*task)
            between = between[share:]

    def o_copy(d, c, src):
        tgt = (hd + d) % 4
        start = pl.multiple_of(src * COLS + c * TAIL, TAIL)
        return pltpu.make_async_remote_copy(
            src_ref=o_out.at[tgt, :, pl.ds(c * TAIL, TAIL)], dst_ref=out_ref.at[:, pl.ds(start, TAIL)],
            send_sem=o_ss.at[d - 1, c], recv_sem=o_rs.at[d - 1, c],
            device_id=(blk, tgt), device_id_type=MESH)

    def own_copy(c):
        start = pl.multiple_of(hd * COLS + c * TAIL, TAIL)
        return pltpu.make_async_copy(
            o_out.at[hd, :, pl.ds(c * TAIL, TAIL)], out_ref.at[:, pl.ds(start, TAIL)], o_ss.at[3, c])

    def finish(c):
        for i in range(c * TAIL // SPAN, (c + 1) * TAIL // SPAN):
            cols = slice(i * SPAN, (i + 1) * SPAN)
            low = (acc_lo[0:SPAN, cols] * (1.0 / acc_lo[SPAN : SPAN + 1, cols])).T
            high = (acc_hi[0:SPAN, cols] * (1.0 / acc_hi[SPAN : SPAN + 1, cols])).T
            first = jnp.where(pick, low, high).astype(BF16)
            second_rows = jnp.where(pick, high, low).astype(BF16)
            o_out[0, :, cols] = first[:PART]
            o_out[1, :, cols] = first[PART:]
            o_out[2, :, cols] = second_rows[:PART]
            o_out[3, :, cols] = second_rows[PART:]
        for d in (2, 1, 3):
            o_copy(d, c, hd).start()
        own_copy(c).start()

    def ring(t, p):
        return [(t, p, i) for i in (0, 3, 1, 2)]

    def take(tasks):
        for task in tasks:
            arrive(*task)

    take(ring(0, 3)[:1] + ring(0, 1)[:1] + ring(1, 3)[:1] + ring(1, 1)[:1])
    prepare_queries()
    diagonal()
    stage(0, 0, 0)
    take(ring(0, 3)[1:] + ring(0, 1)[1:] + ring(1, 3)[1:] + ring(1, 1)[1:])
    stage(1, 0, 1)
    stage(0, 3, 0)
    stage(1, 3, 1)
    take(ring(0, 2))
    take(ring(1, 2))
    stage(0, 1, 0)
    stage(1, 1, 1)
    gather_stage(0, 2, 0)
    gather_stage(1, 2, 1)
    for c, cols in enumerate(tails):
        work(0, cols)
        work(1, cols)
        finish(c)
    def worst(b, carry):
        x = kv[b, 4 * SPAN : ROWS].astype(F32)
        return jnp.maximum(carry, x)

    top = lax.fori_loop(0, 64, worst, jnp.zeros((EXTRA, HEAD_DIM), F32))
    ok_ref[0, 0] = jnp.max(jnp.where(top[4:5] * top[8:9] <= NORM_CAP, 1, 0))

    for d in (1, 2, 3):
        piece_copy(d).wait_send()
        q_copy(d).wait_send()
    for d in range(4):
        layer_copy(d).wait_send()
    for t in (0, 1):
        for d in (1, -1):
            first_copy(t, d).wait_send()
            first_forward(t, d).wait_send()

        @pl.loop(0, 4)
        def _(i):
            for d in (1, -1):
                second_copy(t, i, d).wait_send()
                second_forward(t, i, d).wait_send()
            for p in range(4):
                core_copy(t, p, i).wait_send()
    for c in range(len(tails)):
        own_copy(c).wait()
        for d in (1, 2, 3):
            o_copy(d, c, hd).wait_send()
            o_copy(d, c, (hd + 4 - d) % 4).wait_recv()


def attention(shifted, queries, keys, values, positions):
    vmem = pl.BlockSpec(memory_space=pltpu.VMEM)
    anywhere = pl.BlockSpec(memory_space=pl.ANY)
    dma = pltpu.SemaphoreType.DMA
    wide = NBLK * SPAN
    table = rope_table(HEAD_DIM)
    table = jnp.asarray(np.tile(np.concatenate([table, table])[None], (8, 1)))
    return pl.pallas_call(
        functools.partial(fused, shifted),
        out_shape=(
            jax.ShapeDtypeStruct((PART, QHEADS * HEAD_DIM), BF16),
            jax.ShapeDtypeStruct((1, 1), jnp.int32),
        ),
        in_specs=[anywhere] * 5,
        out_specs=(anywhere, pl.BlockSpec(memory_space=pltpu.SMEM)),
        scratch_shapes=[
            pltpu.VMEM((PART, QHEADS * HEAD_DIM), BF16),
            pltpu.VMEM((PART, KVHEADS * HEAD_DIM), BF16),
            pltpu.VMEM((PART, KVHEADS * HEAD_DIM), BF16),
            pltpu.SMEM((PART,), jnp.int32),
            pltpu.VMEM((8, HEAD_DIM), F32),
            pltpu.VMEM((64, ROWS, HEAD_DIM), BF16),
            pltpu.VMEM((4, PIECE, HEAD_DIM), BF16),
            pltpu.VMEM((4, PIECE, HEAD_DIM), BF16),
            pltpu.VMEM((4, PIECE, HEAD_DIM), BF16),
            pltpu.VMEM((4, GROUP * PART, HEAD_DIM), BF16),
            pltpu.VMEM((4, GROUP * PART, HEAD_DIM), BF16),
            pltpu.VMEM((2 * HEAD_DIM, COLS), BF16),
            pltpu.VMEM((2, wide, HEAD_DIM), BF16),
            pltpu.VMEM((2, wide, 2 * HEAD_DIM), BF16),
            pltpu.VMEM((2, SPAN + EXTRA, wide), BF16),
            pltpu.VMEM((2, 2 * SPAN + EXTRA, wide), BF16),
            pltpu.VMEM((2, NBLK, EXTRA, HEAD_DIM), F32),
            pltpu.VMEM((SPAN + 8, COLS), F32),
            pltpu.VMEM((SPAN + 8, COLS), F32),
            pltpu.VMEM((8, COLS), F32),
            pltpu.VMEM((8, COLS), F32),
            pltpu.VMEM((4, PART, COLS), BF16),
            dma((5,)), dma((3,)), dma((3,)), dma((3,)), dma((3,)),
            dma((4, COLS // TAIL)), dma((3, COLS // TAIL)),
            dma((32, 2)), dma((32,)), dma((32,)), dma((8,)), dma((32,)), dma((4,)), dma((4,)),
        ],
        compiler_params=pltpu.CompilerParams(
            collective_id=int(shifted), has_side_effects=True, vmem_limit_bytes=48 * 1024 * 1024
        ),
    )(queries, keys, values, positions, table)


def body(queries, keys, values, positions):
    quick, fine = attention(False, queries, keys, values, positions)
    return lax.cond(
        fine[0, 0] == 1,
        lambda: quick,
        lambda: attention(True, queries, keys, values, positions)[0],
    )


def solution(mesh):
    return jax.shard_map(
        body,
        mesh=mesh,
        in_specs=(
            P(("blk", "head"), None),
            P(("blk", "head"), None),
            P(("blk", "head"), None),
            P(("blk", "head")),
        ),
        out_specs=P(("blk", "head"), None),
        check_vma=False,
    )
```
